512 devices in a mesh: prompt: 16 (over z), resp: 16 (over y_lo, x, core), tp: 2 (over y_hi).
Axes of the slice: x: 4, y: 4 (y_hi: 2, y_lo: 2; y = y_hi * 2 + y_lo), z: 16, core: 2. Of those that a mesh axis runs over, the one named last changes fastest.
Arguments:
- prefix_query: bfloat16 [32768, 5120], P(('prompt', 'resp'), 'tp'), parts along dimension 0, may hold values from -8 to 8
- prefix_cache: bfloat16 [2, 32768, 1024], P(None, ('prompt', 'resp', 'tp')), parts along dimension 1, may hold values from -8 to 8
- response_query: bfloat16 [256, 256, 5120], P(('prompt', 'resp'), None, 'tp'), parts along dimension 0, may hold values from -8 to 8
- response_key_value_cache: bfloat16 [2, 256, 256, 1024], P(None, ('prompt', 'resp'), None, 'tp'), parts along dimension 1, may hold values from -6 to 6
- response_tiles: int32 [256], P(('prompt', 'resp')), parts along dimension 0, may hold values from 1 to 2, as said below
- prefix_mask: int32 [256, 2, 16], P(('prompt', 'resp')), parts along dimension 0, may hold values 0 or 1
- self_mask: int32 [256, 2, 2], P(('prompt', 'resp')), parts along dimension 0, may hold values 0 or 1
Outputs:
- prefix_attended: bfloat16 [32768, 5120], P(('prompt', 'resp'), 'tp'), parts along dimension 0
- response_attended: bfloat16 [256, 256, 5120], P(('prompt', 'resp'), None, 'tp'), parts along dimension 0
The draws below stay inside these ranges and needn't reach their ends.
There are 16 independent parts, one for each index of `prompt`. The reference program is written for one: setup_inputs(seed, part) draws one part's arguments, and reference() takes and returns one part's arrays. A program takes and returns all parts, laid end to end along the dimension named above; each array names one. Nothing has to cross between parts.
Inputs may be any that keep to these rules, and one draw needn't show every extreme that they name: `response_tiles`: at least one response of every prompt has exactly 2 live tiles, and at least one other has exactly 1. `self_mask`: only entries of tiles before the query's tile are read.
All inputs are finite; a program needn't handle non-finite values. No bound on the sum of `prefix_mask` or of `self_mask` on one device may be relied on, other than what follows from the above.
Results may differ from the reference program's by a relative error of at most 0.009.
Values may be sent and summed in bfloat16 or wider, within the bound.
No kernel may reach another device: no remote copies, remote signals or barrier semaphores. Data moves between devices by JAX's collectives and lax.ppermute only.
A program may use at most 128 MiB of HBM per device.

```python
import jax
import jax.numpy as jnp
from jax import lax

QUERY_HEADS = 40
KEY_VALUE_HEADS = 8
HEAD_WIDTH = 128
TILE_TOKENS = 128
LONGEST_TILES = 2
RESPONSE_COUNT = 16
PROMPT_TOKENS = 2048
PT = 16


def draw_prefix_query(key, part):
    key = jax.random.fold_in(key, 1)
    sampled_draw = jax.random.truncated_normal(key, -6.0, 6.0, (PROMPT_TOKENS, QUERY_HEADS * HEAD_WIDTH), jnp.float32)
    return sampled_draw.astype(jnp.bfloat16)


def draw_response_query(key, part):
    key = jax.random.fold_in(key, 2)
    sampled_draw = jax.random.truncated_normal(key, -6.0, 6.0, (RESPONSE_COUNT, LONGEST_TILES * TILE_TOKENS, QUERY_HEADS * HEAD_WIDTH), jnp.float32)
    return sampled_draw.astype(jnp.bfloat16)


def draw_prefix_cache(key, part):
    key = jax.random.fold_in(key, 3)
    sampled_draw = jax.random.truncated_normal(key, -6.0, 6.0, (2, PROMPT_TOKENS, KEY_VALUE_HEADS * HEAD_WIDTH), jnp.float32)
    return sampled_draw.astype(jnp.bfloat16)


def draw_response_tiles(key, part):
    key = jax.random.fold_in(key, 4)
    key_total, key_longest, key_offset = jax.random.split(key, 3)
    tile_counts = jax.random.randint(key_total, (RESPONSE_COUNT,), 1, LONGEST_TILES + 1)
    longest = jax.random.randint(key_longest, (), 0, RESPONSE_COUNT)
    shortest = (longest + jax.random.randint(key_offset, (), 1, RESPONSE_COUNT)) % RESPONSE_COUNT
    positions = jnp.arange(RESPONSE_COUNT)
    tile_counts = jnp.where(positions == shortest, 1, tile_counts)
    return jnp.where(positions == longest, LONGEST_TILES, tile_counts).astype(jnp.int32)


def plant(result, key, low, largest):
    shape = result.shape
    place = [jax.random.randint(jax.random.fold_in(key, axis), (), 0, shape[axis]) for axis in range(len(shape))]
    result = result.at[tuple(place)].set(low)
    longest = shape.index(max(shape))
    place[longest] = (place[longest] + 1) % shape[longest]
    return result.at[tuple(place)].set(largest)


def steps_of(own_key, dims, cuts, smallest, high):
    gain, own = 1.0, jax.random.fold_in(own_key, 6)
    for position, shards_of in cuts:
        draws = jnp.exp(jax.random.uniform(jax.random.fold_in(own, position), (shards_of,), jnp.float32, smallest / len(cuts), high / len(cuts)))
        gain = gain * jnp.repeat(draws, dims[position] // shards_of).reshape([-1 if axis == position else 1 for axis in range(len(dims))])
    return gain


def bell_draw(rng, shape, width, reach, cuts=(), held_as=jnp.bfloat16):
    values = width * jax.random.normal(rng, shape, jnp.float32)
    if cuts:
        values = values * steps_of(rng, shape, cuts, -0.22, 0.18)
    return jnp.clip(values, -reach, reach).astype(held_as)


def setup_inputs(seed: int = 0, part: int = 0) -> dict:
    arg_keys = jax.random.split(jax.random.key(seed), 8)
    part_splits = jax.random.split(jax.random.fold_in(arg_keys[7], part), 8)
    return {
        "prefix_query": draw_prefix_query(jax.random.fold_in(jax.random.fold_in(arg_keys[7], part), 71), part),
        "prefix_cache": draw_prefix_cache(jax.random.fold_in(jax.random.fold_in(arg_keys[7], part), 71), part),
        "response_query": draw_response_query(jax.random.fold_in(jax.random.fold_in(arg_keys[7], part), 71), part),
        "response_key_value_cache": bell_draw(part_splits[3], (2, RESPONSE_COUNT, LONGEST_TILES * TILE_TOKENS, KEY_VALUE_HEADS * HEAD_WIDTH), 1.0, 6.0, ((1, 16), (3, 2))),
        "response_tiles": draw_response_tiles(jax.random.fold_in(jax.random.fold_in(arg_keys[7], part), 71), part),
        "prefix_mask": plant((jax.random.randint(part_splits[5], (RESPONSE_COUNT, LONGEST_TILES, PT), 0, 4) < 3).astype(jnp.int32), jax.random.fold_in(part_splits[5], 1), 0, 1),
        "self_mask": plant((jax.random.randint(part_splits[6], (RESPONSE_COUNT, LONGEST_TILES, LONGEST_TILES), 0, 2) < 1).astype(jnp.int32), jax.random.fold_in(part_splits[6], 1), 0, 1),
    }


NEG_FILL = -1e30


def attend(query_rows, key_matrix, value_matrix, visible):
    row_number = query_rows.shape[0]
    key_total = key_matrix.shape[0]
    group_members = QUERY_HEADS // KEY_VALUE_HEADS
    query_broadcast = query_rows.astype(jnp.float32).reshape(row_number, KEY_VALUE_HEADS, group_members, HEAD_WIDTH)
    key_broadcast = key_matrix.astype(jnp.float32).reshape(key_total, KEY_VALUE_HEADS, HEAD_WIDTH)
    value_broadcast = value_matrix.astype(jnp.float32).reshape(key_total, KEY_VALUE_HEADS, HEAD_WIDTH)
    scores = jnp.einsum("rghd,kgd->ghrk", query_broadcast, key_broadcast, precision=lax.Precision.HIGHEST) * (HEAD_WIDTH ** -0.5)
    row_max = jnp.max(jnp.where(visible, scores, NEG_FILL), axis=-1, keepdims=True)
    weights = jnp.where(visible, jnp.exp(scores - row_max), 0.0)
    totals = jnp.sum(weights, axis=-1)
    rounded = weights.astype(jnp.bfloat16).astype(jnp.float32)
    summed = jnp.einsum("ghrk,kgd->rghd", rounded, value_broadcast, precision=lax.Precision.HIGHEST)
    return summed, totals


def reference(prefix_query, prefix_cache, response_query, response_key_value_cache, response_tiles, prefix_mask, self_mask):
    prompt_pos = jnp.arange(PROMPT_TOKENS, dtype=jnp.int32)
    prompt_visible = prompt_pos[None, :] <= prompt_pos[:, None]
    summed, totals = attend(prefix_query, prefix_cache[0], prefix_cache[1], prompt_visible)
    prefix_attended = (summed / jnp.transpose(totals, (2, 0, 1))[..., None]).astype(jnp.bfloat16)
    prefix_attended = prefix_attended.reshape(PROMPT_TOKENS, QUERY_HEADS * HEAD_WIDTH)
    response_len = LONGEST_TILES * TILE_TOKENS
    row_pos = jnp.arange(response_len, dtype=jnp.int32)
    row_tile = row_pos // TILE_TOKENS
    key_tile = prompt_pos // TILE_TOKENS

    def one_response(inputs):
        query_rows, own_keys, own_values, tile_total, tile_mask, own_mask = inputs
        live_rows = row_tile < tile_total
        prompt_seen = (tile_mask[row_tile][:, key_tile] == 1) & live_rows[:, None]
        causal = row_pos[None, :] <= row_pos[:, None]
        same_tile = row_tile[None, :] == row_tile[:, None]
        earlier_seen = own_mask[row_tile][:, row_tile] == 1
        own_seen = causal & (same_tile | earlier_seen) & live_rows[:, None]
        key_matrix = jnp.concatenate([prefix_cache[0], own_keys], axis=0)
        value_matrix = jnp.concatenate([prefix_cache[1], own_values], axis=0)
        visible = jnp.concatenate([prompt_seen, own_seen], axis=1)
        summed_rows, total_rows = attend(query_rows, key_matrix, value_matrix, visible)
        divisor = jnp.where(live_rows[None, None, :], total_rows, 1.0)
        scaled = summed_rows / jnp.transpose(divisor, (2, 0, 1))[..., None]
        scaled = jnp.where(live_rows[:, None, None, None], scaled, 0.0)
        return scaled.astype(jnp.bfloat16).reshape(response_len, QUERY_HEADS * HEAD_WIDTH)

    response_attended = lax.map(one_response, (response_query, response_key_value_cache[0], response_key_value_cache[1], response_tiles, prefix_mask, self_mask))
    return prefix_attended, response_attended
```

```python
import functools
import math

import jax
import jax.numpy as jnp
from jax import lax
from jax.experimental import pallas as pl
from jax.experimental.pallas import tpu as pltpu
from jax.sharding import PartitionSpec as P

QUERY_HEADS = 40
KEY_VALUE_HEADS = 8
HEAD_WIDTH = 128
TILE = 128
MEMBERS = QUERY_HEADS // KEY_VALUE_HEADS
GROUPS = KEY_VALUE_HEADS // 2
HALF = GROUPS * HEAD_WIDTH
PROMPT_TILES = 16
OWN_TILES = 2
KEY_TILES = PROMPT_TILES + OWN_TILES
PART = 64
ROWS = MEMBERS * TILE
SCALE = HEAD_WIDTH**-0.5
SCALE2 = SCALE * math.log2(math.e)
NEG_FILL = -1e30
AX = ("resp", "tp")
SIZES = (8, 12, 14, 16, 18)
CHUNK = 4


def rank_of(x, y, core):
    return (((y % 2) * 4 + x) * 2 + core) * 2 + y // 2


def pairs(flip):
    return [
        (rank_of(x, y, core), rank_of(*flip(x, y, core)))
        for x in range(4)
        for y in range(4)
        for core in range(2)
    ]


def first_pairs(m):
    return pairs(lambda x, y, core: (x, y ^ m, core) if core == 0 else (x ^ m, y, core))


def second_pairs(m):
    return pairs(lambda x, y, core: (x ^ m, y, core) if core == 0 else (x, y ^ m, core))


CORE_PAIRS = pairs(lambda x, y, core: (x, y, 1 - core))


def gather_prompt(cache, half, core):
    got = [cache] + [lax.ppermute(cache, AX, first_pairs(m)) for m in (1, 2, 3)]
    stacked = jnp.stack(got)
    mine = lax.dynamic_slice_in_dim(stacked, half * HALF, HALF, 3)
    far = jnp.where(core == 0, half, 1 - half)
    other = lax.dynamic_slice_in_dim(stacked, far * HALF, HALF, 3)
    same_core = [mine] + [
        lax.ppermute(mine if m == 1 else other, AX, second_pairs(m)) for m in (1, 2, 3)
    ]
    other_core = [lax.ppermute(a, AX, CORE_PAIRS) for a in same_core]
    return same_core, other_core


def attend_kernel(
    place,
    prefix_mask,
    self_mask,
    prefix_q,
    response_q,
    own_kv,
    *rest,
):
    pieces = rest[:8]
    prefix_out, response_out = rest[8:10]
    keys, values, values_t, queries, sums, acc, row_max, row_sum, lists, counts = rest[10:]
    x, y, core, rank, live = (place[i] for i in range(5))

    @pl.when(pl.program_id(0) == 0)
    def _():
        for t in range(3):
            for i in range(KEY_TILES):
                lists[t, i] = jnp.int32(0)
            lists[t, 0] = rank if t == 0 else jnp.int32(PROMPT_TILES + t - 1)

            def put(seen, tile, count, t=t):
                lists[t, count] = tile
                return count + jnp.where(seen, 1, 0)

            def step(j, count, t=t, put=put):
                seen = j < rank if t == 0 else prefix_mask[t - 1, j] == 1
                return put(seen, j, count)

            count = lax.fori_loop(0, PROMPT_TILES, step, jnp.int32(1))
            if t == 2:
                count = put(self_mask[1, 0] == 1, PROMPT_TILES, count)
            counts[t] = count

    for index, piece in enumerate(pieces):
        from_core = core if index < 4 else 1 - core
        m = index % 4
        for j in range(4):
            source_x = jnp.where(from_core == 0, x ^ m, x ^ j)
            source_y = jnp.where(from_core == 0, y ^ j, y ^ m)
            tile = ((source_y & 1) * 4 + source_x) * 2 + from_core
            start = pl.multiple_of((source_y >> 1) * PART, PART)
            keys[tile, pl.ds(start, PART), :] = piece[j, 0]
            values[tile, pl.ds(start, PART), :] = piece[j, 1]
    for i in range(OWN_TILES):
        keys[PROMPT_TILES + i] = own_kv[0, i * TILE : (i + 1) * TILE, :]
        values[PROMPT_TILES + i] = own_kv[1, i * TILE : (i + 1) * TILE, :]
    for i in range(KEY_TILES):
        values_t[i] = values[i].T
    for t in range(3):
        for h in range(MEMBERS):
            columns = slice(h * HEAD_WIDTH, (h + 1) * HEAD_WIDTH)
            block = prefix_q[:, columns] if t == 0 else response_q[(t - 1) * TILE : t * TILE, columns]
            queries[t, h * TILE : (h + 1) * TILE, :] = block

    def store(t, h, block):
        columns = slice(h * HEAD_WIDTH, (h + 1) * HEAD_WIDTH)

        @pl.when(t == 0)
        def _():
            prefix_out[:, columns] = block

        @pl.when(t > 0)
        def _():
            start = pl.multiple_of((t - 1) * TILE, TILE)
            response_out[pl.ds(start, TILE), columns] = block

    def scores(a, b):
        return lax.dot_general(a, b, (((1,), (1,)), ((), ())), preferred_element_type=jnp.float32)

    def attend(t, size, sure):
        count = counts[t]
        q = queries[t]
        tiles = [lists[t, i] for i in range(size)]
        causal = lax.broadcasted_iota(jnp.int32, (TILE, TILE), 0) <= lax.broadcasted_iota(
            jnp.int32, (TILE, TILE), 1
        )
        causal = jnp.concatenate([causal] * MEMBERS, axis=1)
        weights, total = [], None
        for start in range(0, size, CHUNK):
            chunk = range(start, min(start + CHUNK, size))
            k = jnp.concatenate([keys[tiles[i]] for i in chunk], axis=0)
            part = jnp.exp2(scores(k, q) * SCALE2)
            for i in chunk:
                block = part[(i - start) * TILE : (i - start + 1) * TILE]
                if i == 0:
                    block = jnp.where(causal, block, 0.0)
                elif i >= sure:
                    block = jnp.where(i < count, block, 0.0)
                folded = jnp.sum(block.reshape(TILE // 8, 8, ROWS), axis=0)
                total = folded if total is None else total + folded
                weights.append(block.astype(jnp.bfloat16))
        v = jnp.concatenate([values_t[tile] for tile in tiles], axis=1)
        summed = jnp.dot(v, jnp.concatenate(weights, axis=0), preferred_element_type=jnp.float32)
        total = jnp.sum(total, axis=0, keepdims=True)
        sums[0:1, :] = jnp.minimum(sums[0:1, :], total)
        sums[1:2, :] = jnp.maximum(sums[1:2, :], total)
        done = summed / total
        for h in range(MEMBERS):
            store(t, h, done[:, h * TILE : (h + 1) * TILE].T.astype(jnp.bfloat16))

    def attend_by_maximum(t):
        row_max[...] = jnp.full(row_max.shape, NEG_FILL, jnp.float32)
        row_sum[...] = jnp.zeros(row_sum.shape, jnp.float32)
        acc[...] = jnp.zeros(acc.shape, jnp.float32)
        row = lax.broadcasted_iota(jnp.int32, (TILE, TILE), 0)
        column = lax.broadcasted_iota(jnp.int32, (TILE, TILE), 1)

        @pl.loop(0, counts[t])
        def _(i):
            tile = lists[t, i]
            k, v = keys[tile], values[tile]
            visible = (column <= row) | (i > 0)
            for h in range(MEMBERS):
                rows = slice(h * TILE, (h + 1) * TILE)
                scaled = scores(queries[t, rows, :], k) * SCALE
                before = row_max[rows, :]
                block_max = jnp.max(jnp.where(visible, scaled, NEG_FILL), axis=1, keepdims=True)
                after = jnp.maximum(before, block_max)
                weights = jnp.where(visible, jnp.exp(scaled - after), 0.0)
                factor = jnp.exp(before - after)
                row_sum[rows, :] = row_sum[rows, :] * factor + jnp.sum(weights, axis=1, keepdims=True)
                update = jnp.dot(weights.astype(jnp.bfloat16), v, preferred_element_type=jnp.float32)
                acc[rows, :] = acc[rows, :] * factor + update
                row_max[rows, :] = after

        for h in range(MEMBERS):
            rows = slice(h * TILE, (h + 1) * TILE)
            store(t, h, (acc[rows, :] / row_sum[rows, :]).astype(jnp.bfloat16))

    @pl.when(live < 2)
    def _():
        response_out[TILE:, :] = jnp.zeros((TILE, ROWS), jnp.bfloat16)

    sums[...] = jnp.ones(sums.shape, jnp.float32)
    row_tiles = jnp.where(live == 2, 3, 2)

    @pl.loop(0, row_tiles)
    def _(t):
        count = counts[t]
        for sure, size in zip((1,) + SIZES, SIZES):

            @pl.when((count <= size) if sure == 1 else (count > sure) & (count <= size))
            def _(sure=sure, size=size):
                attend(t, size, sure)

    fits = (jnp.min(sums[0:1, :]) > 1e-25) & (jnp.max(sums[1:2, :]) < 1e30)

    @pl.when(jnp.logical_not(fits))
    def _():
        @pl.loop(0, row_tiles)
        def _(t):
            attend_by_maximum(t)


def attend_local(place, prefix_mask, self_mask, prefix_q, response_q, own_kv, pieces):
    smem = pl.BlockSpec(memory_space=pltpu.SMEM)
    wide = MEMBERS * HEAD_WIDTH
    rows_p, rows_r = prefix_q.shape[0], response_q.shape[0]
    return pl.pallas_call(
        attend_kernel,
        grid=(GROUPS,),
        in_specs=[
            smem,
            smem,
            smem,
            pl.BlockSpec((rows_p, wide), lambda g: (0, g)),
            pl.BlockSpec((rows_r, wide), lambda g: (0, g)),
            pl.BlockSpec((2, rows_r, HEAD_WIDTH), lambda g: (0, 0, g)),
        ]
        + [pl.BlockSpec((4, 2, PART, HEAD_WIDTH), lambda g: (0, 0, 0, g))] * 8,
        out_specs=[
            pl.BlockSpec((rows_p, wide), lambda g: (0, g)),
            pl.BlockSpec((rows_r, wide), lambda g: (0, g)),
        ],
        out_shape=[
            jax.ShapeDtypeStruct(prefix_q.shape, jnp.bfloat16),
            jax.ShapeDtypeStruct(response_q.shape, jnp.bfloat16),
        ],
        scratch_shapes=[
            pltpu.VMEM((KEY_TILES, TILE, HEAD_WIDTH), jnp.bfloat16),
            pltpu.VMEM((KEY_TILES, TILE, HEAD_WIDTH), jnp.bfloat16),
            pltpu.VMEM((KEY_TILES, HEAD_WIDTH, TILE), jnp.bfloat16),
            pltpu.VMEM((3, ROWS, HEAD_WIDTH), jnp.bfloat16),
            pltpu.VMEM((8, ROWS), jnp.float32),
            pltpu.VMEM((ROWS, HEAD_WIDTH), jnp.float32),
            pltpu.VMEM((ROWS, HEAD_WIDTH), jnp.float32),
            pltpu.VMEM((ROWS, HEAD_WIDTH), jnp.float32),
            pltpu.SMEM((3, KEY_TILES + 2), jnp.int32),
            pltpu.SMEM((3,), jnp.int32),
        ],
        compiler_params=pltpu.CompilerParams(vmem_limit_bytes=40 * 1024 * 1024),
        cost_estimate=pl.CostEstimate(
            flops=8 * 10**9, bytes_accessed=8 * 10**6, transcendentals=15 * 10**6
        ),
    )(place, prefix_mask, self_mask, prefix_q, response_q, own_kv, *pieces)


def shards(
    prefix_query,
    prefix_cache,
    response_query,
    response_key_value_cache,
    response_tiles,
    prefix_mask,
    self_mask,
):
    rank = lax.axis_index("resp")
    half = lax.axis_index("tp")
    core = rank % 2
    x = (rank // 2) % 4
    y = half * 2 + rank // 8
    place = jnp.stack([x, y, core, rank, response_tiles[0]]).astype(jnp.int32)
    same_core, other_core = gather_prompt(prefix_cache, half, core)
    prefix_out, response_out = attend_local(
        place,
        prefix_mask[0],
        self_mask[0],
        prefix_query,
        response_query[0],
        response_key_value_cache[:, 0],
        same_core + other_core,
    )
    return prefix_out, response_out[None]


def solution(mesh):
    placed = (
        P(("prompt", "resp"), "tp"),
        P(None, ("prompt", "resp", "tp"), None),
        P(("prompt", "resp"), None, "tp"),
        P(None, ("prompt", "resp"), None, "tp"),
        P(("prompt", "resp")),
        P(("prompt", "resp"), None, None),
        P(("prompt", "resp"), None, None),
    )
    return jax.shard_map(
        shards,
        mesh=mesh,
        in_specs=placed,
        out_specs=(P(("prompt", "resp"), "tp"), P(("prompt", "resp"), None, "tp")),
        check_vma=False,
    )
```

```python
import functools
import math

import jax
import jax.numpy as jnp
from jax import lax
from jax.experimental import pallas as pl
from jax.experimental.pallas import tpu as pltpu
from jax.sharding import PartitionSpec as P

QUERY_HEADS = 40
KEY_VALUE_HEADS = 8
HEAD_WIDTH = 128
TILE = 128
MEMBERS = QUERY_HEADS // KEY_VALUE_HEADS
GROUPS = KEY_VALUE_HEADS // 2
HALF = GROUPS * HEAD_WIDTH
PROMPT_TILES = 16
OWN_TILES = 2
KEY_TILES = PROMPT_TILES + OWN_TILES
PART = 64
ROWS = MEMBERS * TILE
SCALE = HEAD_WIDTH**-0.5
SCALE2 = SCALE * math.log2(math.e)
NEG_FILL = -1e30
AX = ("resp", "tp")
SIZES = (8, 12, 14, 16, 18)
CHUNK = 4


def rank_of(x, y, core):
    return (((y % 2) * 4 + x) * 2 + core) * 2 + y // 2


def pairs(flip):
    return [
        (rank_of(x, y, core), rank_of(*flip(x, y, core)))
        for x in range(4)
        for y in range(4)
        for core in range(2)
    ]


def first_pairs(m):
    return pairs(lambda x, y, core: (x, y ^ m, core) if core == 0 else (x ^ m, y, core))


def second_pairs(m):
    return pairs(lambda x, y, core: (x ^ m, y, core) if core == 0 else (x, y ^ m, core))


CORE_PAIRS = pairs(lambda x, y, core: (x, y, 1 - core))


def gather_prompt(cache, half, core):
    got = [cache] + [lax.ppermute(cache, AX, first_pairs(m)) for m in (1, 2, 3)]
    stacked = jnp.stack(got)
    mine = lax.dynamic_slice_in_dim(stacked, half * HALF, HALF, 3)
    far = jnp.where(core == 0, half, 1 - half)
    other = lax.dynamic_slice_in_dim(stacked, far * HALF, HALF, 3)
    same_core = [mine] + [
        lax.ppermute(mine if m == 1 else other, AX, second_pairs(m)) for m in (1, 2, 3)
    ]
    other_core = [lax.ppermute(a, AX, CORE_PAIRS) for a in same_core]
    return same_core, other_core


def attend_kernel(
    place,
    prefix_mask,
    self_mask,
    prefix_q,
    response_q,
    own_kv,
    *rest,
):
    pieces = rest[:8]
    prefix_out, response_out = rest[8:10]
    keys, values, values_t, queries, sums, acc, row_max, row_sum, lists, counts = rest[10:]
    x, y, core, rank, live = (place[i] for i in range(5))

    @pl.when(pl.program_id(0) == 0)
    def _():
        for t in range(3):
            for i in range(KEY_TILES):
                lists[t, i] = jnp.int32(0)
            lists[t, 0] = rank if t == 0 else jnp.int32(PROMPT_TILES + t - 1)

            def put(seen, tile, count, t=t):
                lists[t, count] = tile
                return count + jnp.where(seen, 1, 0)

            def step(j, count, t=t, put=put):
                seen = j < rank if t == 0 else prefix_mask[t - 1, j] == 1
                return put(seen, j, count)

            count = lax.fori_loop(0, PROMPT_TILES, step, jnp.int32(1))
            if t == 2:
                count = put(self_mask[1, 0] == 1, PROMPT_TILES, count)
            counts[t] = count

    for index, piece in enumerate(pieces):
        from_core = core if index < 4 else 1 - core
        m = index % 4
        for j in range(4):
            source_x = jnp.where(from_core == 0, x ^ m, x ^ j)
            source_y = jnp.where(from_core == 0, y ^ j, y ^ m)
            tile = ((source_y & 1) * 4 + source_x) * 2 + from_core
            start = pl.multiple_of((source_y >> 1) * PART, PART)
            keys[tile, pl.ds(start, PART), :] = piece[j, 0]
            values[tile, pl.ds(start, PART), :] = piece[j, 1]
    for i in range(OWN_TILES):
        keys[PROMPT_TILES + i] = own_kv[0, i * TILE : (i + 1) * TILE, :]
        values[PROMPT_TILES + i] = own_kv[1, i * TILE : (i + 1) * TILE, :]
    for i in range(KEY_TILES):
        values_t[i] = values[i].T
    for t in range(3):
        for h in range(MEMBERS):
            columns = slice(h * HEAD_WIDTH, (h + 1) * HEAD_WIDTH)
            block = prefix_q[:, columns] if t == 0 else response_q[(t - 1) * TILE : t * TILE, columns]
            queries[t, h * TILE : (h + 1) * TILE, :] = block

    def store(t, h, block):
        columns = slice(h * HEAD_WIDTH, (h + 1) * HEAD_WIDTH)

        @pl.when(t == 0)
        def _():
            prefix_out[:, columns] = block

        @pl.when(t > 0)
        def _():
            start = pl.multiple_of((t - 1) * TILE, TILE)
            response_out[pl.ds(start, TILE), columns] = block

    def store_all(t, block):
        @pl.when(t == 0)
        def _():
            prefix_out[...] = block

        @pl.when(t > 0)
        def _():
            response_out[pl.ds(pl.multiple_of((t - 1) * TILE, TILE), TILE), :] = block

    def scores(a, b):
        return lax.dot_general(a, b, (((1,), (1,)), ((), ())), preferred_element_type=jnp.float32)

    def attend(t, size, sure):
        count = counts[t]
        q = queries[t]
        tiles = [lists[t, i] for i in range(size)]
        causal = lax.broadcasted_iota(jnp.int32, (TILE, TILE), 0) <= lax.broadcasted_iota(
            jnp.int32, (TILE, TILE), 1
        )
        causal = jnp.concatenate([causal] * MEMBERS, axis=1)
        weights, total = [], None
        for start in range(0, size, CHUNK):
            chunk = range(start, min(start + CHUNK, size))
            k = jnp.concatenate([keys[tiles[i]] for i in chunk], axis=0)
            part = jnp.exp2(scores(k, q) * SCALE2)
            for i in chunk:
                block = part[(i - start) * TILE : (i - start + 1) * TILE]
                if i == 0:
                    block = jnp.where(causal, block, 0.0)
                elif i >= sure:
                    block = jnp.where(i < count, block, 0.0)
                folded = jnp.sum(block.reshape(TILE // 8, 8, ROWS), axis=0)
                total = folded if total is None else total + folded
                weights.append(block.astype(jnp.bfloat16))
        v = jnp.concatenate([values_t[tile] for tile in tiles], axis=1)
        summed = jnp.dot(v, jnp.concatenate(weights, axis=0), preferred_element_type=jnp.float32)
        total = jnp.sum(total, axis=0, keepdims=True)
        sums[0:1, :] = jnp.minimum(sums[0:1, :], total)
        sums[1:2, :] = jnp.maximum(sums[1:2, :], total)
        done = summed / total
        blocks = [done[:, h * TILE : (h + 1) * TILE].T.astype(jnp.bfloat16) for h in range(MEMBERS)]
        store_all(t, jnp.concatenate(blocks, axis=1))

    def attend_by_maximum(t):
        row_max[...] = jnp.full(row_max.shape, NEG_FILL, jnp.float32)
        row_sum[...] = jnp.zeros(row_sum.shape, jnp.float32)
        acc[...] = jnp.zeros(acc.shape, jnp.float32)
        row = lax.broadcasted_iota(jnp.int32, (TILE, TILE), 0)
        column = lax.broadcasted_iota(jnp.int32, (TILE, TILE), 1)

        @pl.loop(0, counts[t])
        def _(i):
            tile = lists[t, i]
            k, v = keys[tile], values[tile]
            visible = (column <= row) | (i > 0)
            for h in range(MEMBERS):
                rows = slice(h * TILE, (h + 1) * TILE)
                scaled = scores(queries[t, rows, :], k) * SCALE
                before = row_max[rows, :]
                block_max = jnp.max(jnp.where(visible, scaled, NEG_FILL), axis=1, keepdims=True)
                after = jnp.maximum(before, block_max)
                weights = jnp.where(visible, jnp.exp(scaled - after), 0.0)
                factor = jnp.exp(before - after)
                row_sum[rows, :] = row_sum[rows, :] * factor + jnp.sum(weights, axis=1, keepdims=True)
                update = jnp.dot(weights.astype(jnp.bfloat16), v, preferred_element_type=jnp.float32)
                acc[rows, :] = acc[rows, :] * factor + update
                row_max[rows, :] = after

        for h in range(MEMBERS):
            rows = slice(h * TILE, (h + 1) * TILE)
            store(t, h, (acc[rows, :] / row_sum[rows, :]).astype(jnp.bfloat16))

    @pl.when(live < 2)
    def _():
        response_out[TILE:, :] = jnp.zeros((TILE, ROWS), jnp.bfloat16)

    sums[...] = jnp.ones(sums.shape, jnp.float32)
    row_tiles = jnp.where(live == 2, 3, 2)

    @pl.loop(0, row_tiles)
    def _(t):
        count = counts[t]
        for sure, size in zip((1,) + SIZES, SIZES):

            @pl.when((count <= size) if sure == 1 else (count > sure) & (count <= size))
            def _(sure=sure, size=size):
                attend(t, size, sure)

    fits = (jnp.min(sums[0:1, :]) > 1e-25) & (jnp.max(sums[1:2, :]) < 1e30)

    @pl.when(jnp.logical_not(fits))
    def _():
        @pl.loop(0, row_tiles)
        def _(t):
            attend_by_maximum(t)


def attend_local(place, prefix_mask, self_mask, prefix_q, response_q, own_kv, pieces):
    smem = pl.BlockSpec(memory_space=pltpu.SMEM)
    wide = MEMBERS * HEAD_WIDTH
    rows_p, rows_r = prefix_q.shape[0], response_q.shape[0]
    return pl.pallas_call(
        attend_kernel,
        grid=(GROUPS,),
        in_specs=[
            smem,
            smem,
            smem,
            pl.BlockSpec((rows_p, wide), lambda g: (0, g)),
            pl.BlockSpec((rows_r, wide), lambda g: (0, g)),
            pl.BlockSpec((2, rows_r, HEAD_WIDTH), lambda g: (0, 0, g)),
        ]
        + [pl.BlockSpec((4, 2, PART, HEAD_WIDTH), lambda g: (0, 0, 0, g))] * 8,
        out_specs=[
            pl.BlockSpec((rows_p, wide), lambda g: (0, g)),
            pl.BlockSpec((rows_r, wide), lambda g: (0, g)),
        ],
        out_shape=[
            jax.ShapeDtypeStruct(prefix_q.shape, jnp.bfloat16),
            jax.ShapeDtypeStruct(response_q.shape, jnp.bfloat16),
        ],
        scratch_shapes=[
            pltpu.VMEM((KEY_TILES, TILE, HEAD_WIDTH), jnp.bfloat16),
            pltpu.VMEM((KEY_TILES, TILE, HEAD_WIDTH), jnp.bfloat16),
            pltpu.VMEM((KEY_TILES, HEAD_WIDTH, TILE), jnp.bfloat16),
            pltpu.VMEM((3, ROWS, HEAD_WIDTH), jnp.bfloat16),
            pltpu.VMEM((8, ROWS), jnp.float32),
            pltpu.VMEM((ROWS, HEAD_WIDTH), jnp.float32),
            pltpu.VMEM((ROWS, HEAD_WIDTH), jnp.float32),
            pltpu.VMEM((ROWS, HEAD_WIDTH), jnp.float32),
            pltpu.SMEM((3, KEY_TILES + 2), jnp.int32),
            pltpu.SMEM((3,), jnp.int32),
        ],
        compiler_params=pltpu.CompilerParams(vmem_limit_bytes=40 * 1024 * 1024),
        cost_estimate=pl.CostEstimate(
            flops=8 * 10**9, bytes_accessed=8 * 10**6, transcendentals=15 * 10**6
        ),
    )(place, prefix_mask, self_mask, prefix_q, response_q, own_kv, *pieces)


def shards(
    prefix_query,
    prefix_cache,
    response_query,
    response_key_value_cache,
    response_tiles,
    prefix_mask,
    self_mask,
):
    rank = lax.axis_index("resp")
    half = lax.axis_index("tp")
    core = rank % 2
    x = (rank // 2) % 4
    y = half * 2 + rank // 8
    place = jnp.stack([x, y, core, rank, response_tiles[0]]).astype(jnp.int32)
    same_core, other_core = gather_prompt(prefix_cache, half, core)
    prefix_out, response_out = attend_local(
        place,
        prefix_mask[0],
        self_mask[0],
        prefix_query,
        response_query[0],
        response_key_value_cache[:, 0],
        same_core + other_core,
    )
    return prefix_out, response_out[None]


def solution(mesh):
    placed = (
        P(("prompt", "resp"), "tp"),
        P(None, ("prompt", "resp", "tp"), None),
        P(("prompt", "resp"), None, "tp"),
        P(None, ("prompt", "resp"), None, "tp"),
        P(("prompt", "resp")),
        P(("prompt", "resp"), None, None),
        P(("prompt", "resp"), None, None),
    )
    return jax.shard_map(
        shards,
        mesh=mesh,
        in_specs=placed,
        out_specs=(P(("prompt", "resp"), "tp"), P(("prompt", "resp"), None, "tp")),
        check_vma=False,
    )
```

```python
import functools
import math

import jax
import jax.numpy as jnp
from jax import lax
from jax.experimental import pallas as pl
from jax.experimental.pallas import tpu as pltpu
from jax.sharding import PartitionSpec as P

QUERY_HEADS = 40
KEY_VALUE_HEADS = 8
HEAD_WIDTH = 128
TILE = 128
MEMBERS = QUERY_HEADS // KEY_VALUE_HEADS
GROUPS = KEY_VALUE_HEADS // 2
HALF = GROUPS * HEAD_WIDTH
PROMPT_TILES = 16
OWN_TILES = 2
KEY_TILES = PROMPT_TILES + OWN_TILES
PART = 64
ROWS = MEMBERS * TILE
SCALE = HEAD_WIDTH**-0.5
SCALE2 = SCALE * math.log2(math.e)
NEG_FILL = -1e30
AX = ("resp", "tp")
SIZES = (8, 10, 12, 13, 14, 15, 16, 17, 18)
CHUNK = 4


def rank_of(x, y, core):
    return (((y % 2) * 4 + x) * 2 + core) * 2 + y // 2


def pairs(flip):
    return [
        (rank_of(x, y, core), rank_of(*flip(x, y, core)))
        for x in range(4)
        for y in range(4)
        for core in range(2)
    ]


def first_pairs(m):
    return pairs(lambda x, y, core: (x, y ^ m, core) if core == 0 else (x ^ m, y, core))


def second_pairs(m):
    return pairs(lambda x, y, core: (x ^ m, y, core) if core == 0 else (x, y ^ m, core))


CORE_PAIRS = pairs(lambda x, y, core: (x, y, 1 - core))


def gather_prompt(cache, half, core):
    far = jnp.where(core == 0, half, 1 - half)

    def columns(block, which):
        return lax.dynamic_slice_in_dim(block, which * HALF, HALF, block.ndim - 1)

    own_mine, own_other = lax.optimization_barrier((columns(cache, half), columns(cache, far)))
    got = jnp.stack([lax.ppermute(cache, AX, first_pairs(m)) for m in (1, 2, 3)])
    mine = jnp.concatenate([own_mine[None], columns(got, half)])
    other = jnp.concatenate([own_other[None], columns(got, far)])
    same_core = [mine] + [
        lax.ppermute(mine if m == 1 else other, AX, second_pairs(m)) for m in (1, 2, 3)
    ]
    other_core = [lax.ppermute(a, AX, CORE_PAIRS) for a in same_core]
    return same_core, other_core


def attend_kernel(
    place,
    prefix_mask,
    self_mask,
    prefix_q,
    response_q,
    own_kv,
    *rest,
):
    pieces = rest[:8]
    prefix_out, response_out = rest[8:10]
    keys, values, values_t, queries, sums, acc, row_max, row_sum, lists, counts = rest[10:]
    x, y, core, rank, live = (place[i] for i in range(5))

    @pl.when(pl.program_id(0) == 0)
    def _():
        for t in range(3):
            for i in range(KEY_TILES):
                lists[t, i] = jnp.int32(0)
            lists[t, 0] = rank if t == 0 else jnp.int32(PROMPT_TILES + t - 1)

            def put(seen, tile, count, t=t):
                lists[t, count] = tile
                return count + jnp.where(seen, 1, 0)

            def step(j, count, t=t, put=put):
                seen = j < rank if t == 0 else prefix_mask[t - 1, j] == 1
                return put(seen, j, count)

            count = lax.fori_loop(0, PROMPT_TILES, step, jnp.int32(1))
            if t == 2:
                count = put(self_mask[1, 0] == 1, PROMPT_TILES, count)
            counts[t] = count

    for index, piece in enumerate(pieces):
        from_core = core if index < 4 else 1 - core
        m = index % 4
        for j in range(4):
            source_x = jnp.where(from_core == 0, x ^ m, x ^ j)
            source_y = jnp.where(from_core == 0, y ^ j, y ^ m)
            tile = ((source_y & 1) * 4 + source_x) * 2 + from_core
            start = pl.multiple_of((source_y >> 1) * PART, PART)
            keys[tile, pl.ds(start, PART), :] = piece[j, 0]
            values[tile, pl.ds(start, PART), :] = piece[j, 1]
    for i in range(OWN_TILES):
        keys[PROMPT_TILES + i] = own_kv[0, i * TILE : (i + 1) * TILE, :]
        values[PROMPT_TILES + i] = own_kv[1, i * TILE : (i + 1) * TILE, :]
    for i in range(KEY_TILES):
        values_t[i] = values[i].T
    for t in range(3):
        for h in range(MEMBERS):
            columns = slice(h * HEAD_WIDTH, (h + 1) * HEAD_WIDTH)
            block = prefix_q[:, columns] if t == 0 else response_q[(t - 1) * TILE : t * TILE, columns]
            queries[t, h * TILE : (h + 1) * TILE, :] = block

    def store(t, h, block):
        columns = slice(h * HEAD_WIDTH, (h + 1) * HEAD_WIDTH)

        @pl.when(t == 0)
        def _():
            prefix_out[:, columns] = block

        @pl.when(t > 0)
        def _():
            start = pl.multiple_of((t - 1) * TILE, TILE)
            response_out[pl.ds(start, TILE), columns] = block

    def store_all(t, block):
        @pl.when(t == 0)
        def _():
            prefix_out[...] = block

        @pl.when(t > 0)
        def _():
            response_out[pl.ds(pl.multiple_of((t - 1) * TILE, TILE), TILE), :] = block

    def scores(a, b):
        return lax.dot_general(a, b, (((1,), (1,)), ((), ())), preferred_element_type=jnp.float32)

    def attend(t, size, sure):
        count = counts[t]
        q = queries[t]
        tiles = [lists[t, i] for i in range(size)]
        causal = lax.broadcasted_iota(jnp.int32, (TILE, TILE), 0) <= lax.broadcasted_iota(
            jnp.int32, (TILE, TILE), 1
        )
        causal = jnp.concatenate([causal] * MEMBERS, axis=1)
        weights, total = [], None
        for start in range(0, size, CHUNK):
            chunk = range(start, min(start + CHUNK, size))
            k = jnp.concatenate([keys[tiles[i]] for i in chunk], axis=0)
            part = jnp.exp2(scores(k, q) * SCALE2)
            for i in chunk:
                block = part[(i - start) * TILE : (i - start + 1) * TILE]
                if i == 0:
                    block = jnp.where(causal, block, 0.0)
                elif i >= sure:
                    block = jnp.where(i < count, block, 0.0)
                folded = jnp.sum(block.reshape(TILE // 8, 8, ROWS), axis=0)
                total = folded if total is None else total + folded
                weights.append(block.astype(jnp.bfloat16))
        v = jnp.concatenate([values_t[tile] for tile in tiles], axis=1)
        summed = jnp.dot(v, jnp.concatenate(weights, axis=0), preferred_element_type=jnp.float32)
        total = jnp.sum(total, axis=0, keepdims=True)
        sums[0:1, :] = jnp.minimum(sums[0:1, :], total)
        sums[1:2, :] = jnp.maximum(sums[1:2, :], total)
        done = summed / total
        blocks = [done[:, h * TILE : (h + 1) * TILE].T.astype(jnp.bfloat16) for h in range(MEMBERS)]
        store_all(t, jnp.concatenate(blocks, axis=1))

    def attend_by_maximum(t):
        row_max[...] = jnp.full(row_max.shape, NEG_FILL, jnp.float32)
        row_sum[...] = jnp.zeros(row_sum.shape, jnp.float32)
        acc[...] = jnp.zeros(acc.shape, jnp.float32)
        row = lax.broadcasted_iota(jnp.int32, (TILE, TILE), 0)
        column = lax.broadcasted_iota(jnp.int32, (TILE, TILE), 1)

        @pl.loop(0, counts[t])
        def _(i):
            tile = lists[t, i]
            k, v = keys[tile], values[tile]
            visible = (column <= row) | (i > 0)
            for h in range(MEMBERS):
                rows = slice(h * TILE, (h + 1) * TILE)
                scaled = scores(queries[t, rows, :], k) * SCALE
                before = row_max[rows, :]
                block_max = jnp.max(jnp.where(visible, scaled, NEG_FILL), axis=1, keepdims=True)
                after = jnp.maximum(before, block_max)
                weights = jnp.where(visible, jnp.exp(scaled - after), 0.0)
                factor = jnp.exp(before - after)
                row_sum[rows, :] = row_sum[rows, :] * factor + jnp.sum(weights, axis=1, keepdims=True)
                update = jnp.dot(weights.astype(jnp.bfloat16), v, preferred_element_type=jnp.float32)
                acc[rows, :] = acc[rows, :] * factor + update
                row_max[rows, :] = after

        for h in range(MEMBERS):
            rows = slice(h * TILE, (h + 1) * TILE)
            store(t, h, (acc[rows, :] / row_sum[rows, :]).astype(jnp.bfloat16))

    @pl.when(live < 2)
    def _():
        response_out[TILE:, :] = jnp.zeros((TILE, ROWS), jnp.bfloat16)

    sums[...] = jnp.ones(sums.shape, jnp.float32)
    row_tiles = jnp.where(live == 2, 3, 2)

    @pl.loop(0, row_tiles)
    def _(t):
        count = counts[t]
        for sure, size in zip((1,) + SIZES, SIZES):

            @pl.when((count <= size) if sure == 1 else (count > sure) & (count <= size))
            def _(sure=sure, size=size):
                attend(t, size, sure)

    fits = (jnp.min(sums[0:1, :]) > 1e-25) & (jnp.max(sums[1:2, :]) < 1e30)

    @pl.when(jnp.logical_not(fits))
    def _():
        @pl.loop(0, row_tiles)
        def _(t):
            attend_by_maximum(t)


def attend_local(place, prefix_mask, self_mask, prefix_q, response_q, own_kv, pieces):
    smem = pl.BlockSpec(memory_space=pltpu.SMEM)
    wide = MEMBERS * HEAD_WIDTH
    rows_p, rows_r = prefix_q.shape[0], response_q.shape[0]
    return pl.pallas_call(
        attend_kernel,
        grid=(GROUPS,),
        in_specs=[
            smem,
            smem,
            smem,
            pl.BlockSpec((rows_p, wide), lambda g: (0, g)),
            pl.BlockSpec((rows_r, wide), lambda g: (0, g)),
            pl.BlockSpec((2, rows_r, HEAD_WIDTH), lambda g: (0, 0, g)),
        ]
        + [pl.BlockSpec((4, 2, PART, HEAD_WIDTH), lambda g: (0, 0, 0, g))] * 8,
        out_specs=[
            pl.BlockSpec((rows_p, wide), lambda g: (0, g)),
            pl.BlockSpec((rows_r, wide), lambda g: (0, g)),
        ],
        out_shape=[
            jax.ShapeDtypeStruct(prefix_q.shape, jnp.bfloat16),
            jax.ShapeDtypeStruct(response_q.shape, jnp.bfloat16),
        ],
        scratch_shapes=[
            pltpu.VMEM((KEY_TILES, TILE, HEAD_WIDTH), jnp.bfloat16),
            pltpu.VMEM((KEY_TILES, TILE, HEAD_WIDTH), jnp.bfloat16),
            pltpu.VMEM((KEY_TILES, HEAD_WIDTH, TILE), jnp.bfloat16),
            pltpu.VMEM((3, ROWS, HEAD_WIDTH), jnp.bfloat16),
            pltpu.VMEM((8, ROWS), jnp.float32),
            pltpu.VMEM((ROWS, HEAD_WIDTH), jnp.float32),
            pltpu.VMEM((ROWS, HEAD_WIDTH), jnp.float32),
            pltpu.VMEM((ROWS, HEAD_WIDTH), jnp.float32),
            pltpu.SMEM((3, KEY_TILES + 2), jnp.int32),
            pltpu.SMEM((3,), jnp.int32),
        ],
        compiler_params=pltpu.CompilerParams(vmem_limit_bytes=40 * 1024 * 1024),
        cost_estimate=pl.CostEstimate(
            flops=8 * 10**9, bytes_accessed=8 * 10**6, transcendentals=15 * 10**6
        ),
    )(place, prefix_mask, self_mask, prefix_q, response_q, own_kv, *pieces)


def shards(
    prefix_query,
    prefix_cache,
    response_query,
    response_key_value_cache,
    response_tiles,
    prefix_mask,
    self_mask,
):
    rank = lax.axis_index("resp")
    half = lax.axis_index("tp")
    core = rank % 2
    x = (rank // 2) % 4
    y = half * 2 + rank // 8
    place = jnp.stack([x, y, core, rank, response_tiles[0]]).astype(jnp.int32)
    same_core, other_core = gather_prompt(prefix_cache, half, core)
    prefix_out, response_out = attend_local(
        place,
        prefix_mask[0],
        self_mask[0],
        prefix_query,
        response_query[0],
        response_key_value_cache[:, 0],
        same_core + other_core,
    )
    return prefix_out, response_out[None]


def solution(mesh):
    placed = (
        P(("prompt", "resp"), "tp"),
        P(None, ("prompt", "resp", "tp"), None),
        P(("prompt", "resp"), None, "tp"),
        P(None, ("prompt", "resp"), None, "tp"),
        P(("prompt", "resp")),
        P(("prompt", "resp"), None, None),
        P(("prompt", "resp"), None, None),
    )
    return jax.shard_map(
        shards,
        mesh=mesh,
        in_specs=placed,
        out_specs=(P(("prompt", "resp"), "tp"), P(("prompt", "resp"), None, "tp")),
        check_vma=False,
    )
```
